256 devices in a mesh: seq: 32 (over x, z), fsdp: 8 (over y, core).
Axes of the slice: x: 4, y: 4, z: 8, core: 2. Of those that a mesh axis runs over, the one named last changes fastest.
Arguments:
- byte_states: bfloat16 [8, 16384, 1024], P('fsdp', 'seq'), may hold values from -6 to 6
- group_states: bfloat16 [8, 4096, 1024], P('fsdp', 'seq'), may hold values from -6 to 6
- boundaries: int32 [8, 4096], P('fsdp'), may hold values from 0 to 16383, as said below
- w_query: bfloat16 [1024, 1024], P('fsdp'), may hold values from -0.1875 to 0.1875
- w_key: bfloat16 [1024, 1024], P('fsdp'), may hold values from -0.1875 to 0.1875
- w_value: bfloat16 [1024, 1024], P('fsdp'), may hold values from -0.1875 to 0.1875
- w_out: bfloat16 [1024, 1024], P('fsdp'), may hold values from -0.75 to 0.75
Outputs:
- dechunked: bfloat16 [8, 16384, 1024], P('fsdp', 'seq')
- attended: bfloat16 [8, 16384, 1024], P('fsdp', 'seq')
The draws below stay inside these ranges and needn't reach their ends.
Inputs may be any that keep to these rules, and one draw needn't show every extreme that they name: Each boundaries[i] rises strictly and starts at 0. Device j along seq holds bytes j * 512 to (j + 1) * 512 - 1 and groups j * 128 to (j + 1) * 128 - 1; the bytes of device j lie in groups j * 128 - 64 to (j + 1) * 128 - 1, for j > 0 the first of them is below j * 128, and in every document some device's first is exactly j * 128 - 64.
All inputs are finite; a program needn't handle non-finite values.
Results may differ from the reference program's by a relative error of at most 0.022.
Values may be sent and summed in bfloat16 or wider, within the bound.
No kernel may reach another device: no remote copies, remote signals or barrier semaphores. Data moves between devices by JAX's collectives and lax.ppermute only.
A program may use at most 128 MiB of HBM per device.

```python
import jax
import jax.numpy as jnp
from jax import lax

D = 1024
HEAD_DIM = 64
W = 2048
TOK_DEV = 512
CH = 128
TAIL = 64
QB = 512
DOCS = 8
LEN = 16384
NCH = 4096


def draw_boundaries(key, part):
    key = jax.random.fold_in(key, 7)
    devices_along = NCH // CH

    def one_document(doc_key):
        drift_key, pick_key, place_key = jax.random.split(doc_key, 3)
        inner_drift = jax.random.randint(drift_key, (devices_along - 1,), 1 - TAIL, 0).astype(jnp.int32)
        chosen = jax.random.randint(pick_key, (), 0, devices_along - 1)
        inner_drift = jnp.where(jnp.arange(devices_along - 1) == chosen, 1 - TAIL, inner_drift).astype(jnp.int32)
        edge_zero = jnp.zeros((1,), jnp.int32)
        drift_all = jnp.concatenate([edge_zero, inner_drift, edge_zero])
        counts = CH + drift_all[1:] - drift_all[:-1]
        leading = (jnp.arange(devices_along) == 0).astype(jnp.int32)
        wanted = counts - leading
        block_keys = jax.random.split(place_key, devices_along)
        block_ranks = jax.vmap(lambda block_key: jax.random.permutation(block_key, TOK_DEV - 1))(block_keys)
        picked = block_ranks < wanted[:, None]
        start_marks = jnp.concatenate([leading[:, None] > 0, picked], axis=1).reshape(-1)
        return jnp.nonzero(start_marks, size=NCH)[0].astype(jnp.int32)
    return jax.vmap(one_document)(jax.random.split(key, DOCS))


def level_of(stream_key, shape, pieces, low, top_value):
    def one(dim, shards_of):
        draws = jax.random.uniform(jax.random.fold_in(jax.random.fold_in(stream_key, 6), dim), (shards_of,), jnp.float32, low / len(pieces), top_value / len(pieces))
        return jnp.repeat(jnp.exp(draws), shape[dim] // shards_of).reshape((-1,) + (1,) * (len(shape) - dim - 1))

    loudness = one(*pieces[0])
    for cut in pieces[1:]:
        loudness = loudness * one(*cut)
    return loudness


def normal_values(stream_key, extent, spread, most, shards=(), kind=jnp.bfloat16):
    array = spread * jax.random.normal(stream_key, extent, jnp.float32)
    if shards:
        array = array * level_of(stream_key, extent, shards, -0.22, 0.18)
    return jnp.clip(array, -most, most).astype(kind)


def setup_inputs(seed: int = 0) -> dict:
    keys = jax.random.split(jax.random.key(seed), 8)
    byte_states = normal_values(keys[0], (DOCS, LEN, D), 1.0, 6.0, ((0, 8), (1, 32)))
    group_states = normal_values(keys[1], (DOCS, NCH, D), 1.0, 6.0, ((0, 8), (1, 32)))
    boundaries = draw_boundaries(jax.random.fold_in(keys[7], 71), 0)
    w_query = normal_values(keys[3], (D, D), D ** -0.5, 0.1875, ((0, 8),))
    w_key = normal_values(keys[4], (D, D), D ** -0.5, 0.1875, ((0, 8),))
    w_value = normal_values(keys[5], (D, D), D ** -0.5, 0.1875, ((0, 8),))
    w_out = normal_values(keys[6], (D, D), (D // 16) ** -0.5, 0.75, ((0, 8),))
    return {"byte_states": byte_states, "group_states": group_states, "boundaries": boundaries, "w_query": w_query, "w_key": w_key, "w_value": w_value, "w_out": w_out}


score_scale = 16.0
norm_eps = 1e-06

def head_norm(matrix, factor):
    row_count = matrix.shape[0]
    per_head = matrix.reshape(row_count, D // HEAD_DIM, HEAD_DIM)
    mean_square = lax.optimization_barrier(jnp.mean(per_head * per_head, axis=-1, keepdims=True))
    return (per_head * lax.rsqrt(mean_square + norm_eps) * factor).reshape(row_count, D)

def attend_block(query_hat, key_hat, value_all, block_start):
    head_count = D // HEAD_DIM
    query_blk = lax.dynamic_slice_in_dim(query_hat, block_start, QB, 0)
    key_blk = lax.dynamic_slice_in_dim(key_hat, block_start, W + QB, 0)
    value_blk = lax.dynamic_slice_in_dim(value_all, block_start, W + QB, 0)
    query_heads = query_blk.astype(jnp.float32).reshape(QB, head_count, HEAD_DIM)
    key_heads = key_blk.astype(jnp.float32).reshape(W + QB, head_count, HEAD_DIM)
    value_heads = value_blk.astype(jnp.float32).reshape(W + QB, head_count, HEAD_DIM)
    scores = jnp.einsum('qhd,khd->hqk', query_heads, key_heads)
    offset = jnp.arange(QB, dtype=jnp.int32)[:, None]
    key_index = jnp.arange(W + QB, dtype=jnp.int32)[None, :]
    allowed = (key_index >= offset) & (key_index <= offset + W) & (block_start + key_index - W >= 0)
    exponent = jnp.where(allowed[None], jnp.exp(scores), 0.0)
    weights = (exponent / lax.optimization_barrier(jnp.sum(exponent, axis=-1, keepdims=True))).astype(jnp.bfloat16)
    context = jnp.einsum('hqk,khd->qhd', weights.astype(jnp.float32), value_heads)
    return context.reshape(QB, D).astype(jnp.bfloat16)

def one_document(doc_inputs, w_query, w_key, w_value, w_out):
    byte_rows, group_rows, start_list = doc_inputs
    positions = jnp.arange(LEN, dtype=jnp.int32)
    group_of = (jnp.searchsorted(start_list, positions, side='right') - 1).astype(jnp.int32)
    lifted = jnp.take(group_rows, group_of, axis=0)
    dechunked = (byte_rows.astype(jnp.float32) + lifted.astype(jnp.float32)).astype(jnp.bfloat16)
    widened = dechunked.astype(jnp.float32)
    normed = (widened * lax.rsqrt(lax.optimization_barrier(jnp.mean(widened * widened, axis=-1, keepdims=True)) + norm_eps)).astype(jnp.bfloat16)
    queries = jnp.dot(normed, w_query, preferred_element_type=jnp.float32)
    keys_raw = jnp.dot(normed, w_key, preferred_element_type=jnp.float32)
    values_raw = jnp.dot(normed, w_value, preferred_element_type=jnp.float32)
    query_hat = head_norm(queries, score_scale / HEAD_DIM).astype(jnp.bfloat16)
    key_hat = head_norm(keys_raw, 1.0).astype(jnp.bfloat16)
    value_all = values_raw.astype(jnp.bfloat16)
    padding = jnp.zeros((W, D), jnp.bfloat16)
    key_hat = jnp.concatenate([padding, key_hat], axis=0)
    value_all = jnp.concatenate([padding, value_all], axis=0)
    block_starts = jnp.arange(LEN // QB, dtype=jnp.int32) * QB
    context = lax.map(lambda block_start: attend_block(query_hat, key_hat, value_all, block_start), block_starts)
    context = context.reshape(LEN, D)
    attended = jnp.dot(context, w_out, preferred_element_type=jnp.float32).astype(jnp.bfloat16)
    return (dechunked, attended)

def reference(byte_states, group_states, boundaries, w_query, w_key, w_value, w_out):
    dechunked, attended = lax.map(lambda doc_inputs: one_document(doc_inputs, w_query, w_key, w_value, w_out), (byte_states, group_states, boundaries))
    return (dechunked, attended)
```

```python
import functools

import jax
import jax.numpy as jnp
from jax import lax
from jax.experimental import pallas as pl
from jax.experimental.pallas import tpu as pltpu
from jax.sharding import PartitionSpec as P

HEAD_DIM = 64
TAIL = 64
PAIR = 2 * HEAD_DIM
QUAD = 2 * PAIR
HALF = 256
EPS = 1e-6
QUERY_FACTOR = 16.0 / HEAD_DIM * 1.4426950408889634
BF = jnp.bfloat16
F32 = jnp.float32
NT = (((1,), (1,)), ((), ()))
VMEM_LIMIT = 40 * 2**20


def params():
    return pltpu.CompilerParams(vmem_limit_bytes=VMEM_LIMIT)


def prep_kernel(row0, order_ref, win_ref, bytes_ref, carried_ref, groups_ref, out_ref, normed_ref, hold):
    rows, width = bytes_ref.shape
    position = row0 + lax.broadcasted_iota(jnp.int32, (rows, TAIL), 0)
    position_own = row0 + lax.broadcasted_iota(jnp.int32, (rows, PAIR), 0)
    start, following = win_ref[0:1, :], win_ref[1:2, :]

    def one_hot(lo, hi, where):
        return ((start[:, lo:hi] <= where) & (following[:, lo:hi] > where)).astype(F32).astype(BF)

    own = groups_ref.shape[0]
    lifted = jnp.dot(one_hot(PAIR, PAIR + own, position_own), groups_ref[...], preferred_element_type=F32)
    lifted += jnp.dot(one_hot(0, TAIL, position), carried_ref[...], preferred_element_type=F32)
    dechunked = (bytes_ref[...].astype(F32) + lifted).astype(BF)
    out_ref[...] = dechunked
    wide = dechunked.astype(F32)
    mean = jnp.sum(wide * wide, axis=-1, keepdims=True) * (1.0 / width)
    hold[...] = (wide * lax.rsqrt(mean + EPS)).astype(BF)
    for r in range(width // PAIR):
        at = pl.multiple_of(order_ref[r] * PAIR, PAIR)
        normed_ref[:, r * PAIR : (r + 1) * PAIR] = hold[:, pl.ds(at, PAIR)]


def prep(row0, order, window, own_bytes, carried, own_groups):
    width = own_bytes.shape[1]
    vmem = pl.BlockSpec(memory_space=pltpu.VMEM)
    shape = jax.ShapeDtypeStruct((HALF, width), BF)
    return pl.pallas_call(
        functools.partial(prep_kernel, row0),
        grid=(1,),
        in_specs=[
            pl.BlockSpec(memory_space=pltpu.SMEM),
            pl.BlockSpec(window.shape, lambda i: (0, 0)),
            pl.BlockSpec((HALF, width), lambda i: (row0 // HALF, 0)),
            pl.BlockSpec(carried.shape, lambda i: (0, 0)),
            pl.BlockSpec(own_groups.shape, lambda i: (0, 0)),
        ],
        out_specs=[pl.BlockSpec((HALF, width), lambda i: (0, 0))] * 2,
        out_shape=[shape, shape],
        scratch_shapes=[pltpu.VMEM((HALF, width), BF)],
        compiler_params=params(),
        cost_estimate=pl.CostEstimate(flops=2 * HALF * 192 * width, bytes_accessed=2**21, transcendentals=HALF),
        name="prep",
    )(order, window, own_bytes, carried, own_groups)


def head_norm(raw, factor):
    n = raw.shape[1]
    row = lax.broadcasted_iota(jnp.int32, (n, n), 0) // HEAD_DIM
    column = lax.broadcasted_iota(jnp.int32, (n, n), 1) // HEAD_DIM
    mean_of_head = jnp.where(row == column, 1.0 / HEAD_DIM, 0.0).astype(BF)
    mean_square = jnp.dot((raw * raw).astype(BF), mean_of_head, preferred_element_type=F32)
    return (raw * (lax.rsqrt(mean_square + EPS) * factor)).astype(BF)


def project(x, parts):
    return jnp.dot(x, jnp.concatenate([p[...] for p in parts], axis=0), preferred_element_type=F32)


def masked(scores, mode):
    weights = jnp.exp2(scores)
    if mode != "full":
        query = lax.broadcasted_iota(jnp.int32, scores.shape, 0)
        key = lax.broadcasted_iota(jnp.int32, scores.shape, 1)
        keep = key <= query if mode == "until" else key >= query
        weights = jnp.where(keep, weights, 0.0)
    return weights.astype(BF)


def attend_quad(query, pieces, add_to, put):
    low_q = lax.broadcasted_iota(jnp.int32, (HALF, PAIR), 1) < HEAD_DIM
    zero = jnp.zeros((HALF, PAIR), BF)
    for pair in range(2):
        lanes = slice(pair * PAIR, (pair + 1) * PAIR)
        rights = []
        for keys, values, ones, _ in pieces:
            v = values[:, lanes]
            rights.append(
                (
                    jnp.concatenate([jnp.where(low_q, v, zero), jnp.where(low_q, ones, zero)], axis=1),
                    jnp.concatenate([jnp.where(low_q, zero, v), jnp.where(low_q, zero, ones)], axis=1),
                )
            )
        for part in range(2):
            rows = slice(part * HALF, (part + 1) * HALF)
            q = query[rows, lanes]
            q_a, q_b = jnp.where(low_q, q, zero), jnp.where(low_q, zero, q)
            left, right = [], []
            for (keys, _, _, modes), (right_a, right_b) in zip(pieces, rights):
                if modes[part] == "none":
                    continue
                k = keys[:, lanes]
                left.append(masked(lax.dot_general(q_a, k, NT, preferred_element_type=F32), modes[part]))
                left.append(masked(lax.dot_general(q_b, k, NT, preferred_element_type=F32), modes[part]))
                right += [right_a, right_b]
            total = jnp.dot(
                jnp.concatenate(left, axis=1), jnp.concatenate(right, axis=0), preferred_element_type=F32
            )
            put(pair, rows, total if add_to is None else add_to[pair, rows, :] + total)


def own_kernel(*refs):
    top_ref, bottom_ref = refs[0:2]
    w_q, w_k, w_v = refs[2:10], refs[10:18], refs[18:26]
    query_ref, total_ref = refs[26:]
    x = jnp.concatenate([top_ref[...], bottom_ref[...]], axis=0)
    query = head_norm(project(x, w_q), QUERY_FACTOR)
    query_ref[...] = query
    key = head_norm(project(x, w_k), 1.0)
    value = project(x, w_v).astype(BF)
    ones = jnp.ones((HALF, PAIR), BF)
    pieces = [
        (key[:HALF], value[:HALF], ones, ("until", "full")),
        (key[HALF:], value[HALF:], ones, ("none", "until")),
    ]

    def put(pair, rows, total):
        total_ref[pair, rows, :] = total

    attend_quad(query, pieces, None, put)


def step_body(modes, valid_ref, a_ref, b_ref, w_k, w_v, query_ref, total_ref, put):
    pieces = []
    for i, x_ref in enumerate((a_ref, b_ref)):
        x = x_ref[...]
        valid = valid_ref[i] > 0
        key = head_norm(project(x, w_k), 1.0)
        value = jnp.where(valid, project(x, w_v), 0.0).astype(BF)
        ones = jnp.where(valid, jnp.ones((HALF, PAIR), F32), 0.0).astype(BF)
        pieces.append((key, value, ones, modes[i]))
    attend_quad(query_ref[...], pieces, total_ref, put)


def step_kernel(modes, *refs):
    valid_ref, a_ref, b_ref = refs[0:3]
    query_ref, total_ref, out_ref = refs[19:]

    def put(pair, rows, total):
        out_ref[pair, rows, :] = total

    step_body(modes, valid_ref, a_ref, b_ref, refs[3:11], refs[11:19], query_ref, total_ref, put)


def last_kernel(modes, *refs):
    valid_ref, order_ref, a_ref, b_ref = refs[0:4]
    w_k, w_v, w_o = refs[4:12], refs[12:20], refs[20:28]
    query_ref, total_ref, out_ref, context = refs[28:]
    g = pl.program_id(0)

    def put(pair, rows, total):
        context[2 * g + pair, rows, :] = (total[:, :PAIR] / total[:, PAIR:]).astype(BF)

    step_body(modes, valid_ref, a_ref, b_ref, w_k, w_v, query_ref, total_ref, put)

    @pl.when(g == pl.num_programs(0) - 1)
    def _():
        x = jnp.concatenate([context[order_ref[r]] for r in range(8)], axis=1)
        out_ref[...] = project(x, w_o).astype(BF)


def weight_specs(weights, kind):
    arrays = [part[kind][0] for part in weights]
    specs = [
        pl.BlockSpec((PAIR, QUAD), functools.partial(lambda row, g: (row, g), part[kind][1])) for part in weights
    ]
    return arrays, specs


def fixed(shape):
    return pl.BlockSpec(shape, lambda g: (0,) * len(shape))


def attention_cost(keys, projections):
    flops = 2 * 512 * keys * 1024 * 2 + 2 * 1024 * 1024 * projections
    return pl.CostEstimate(flops=2 * flops, bytes_accessed=14 * 2**20, transcendentals=512 * keys * 16)


def attend_own(top, bottom, weights):
    width = top.shape[1]
    q, q_specs = weight_specs(weights, 0)
    k, k_specs = weight_specs(weights, 1)
    v, v_specs = weight_specs(weights, 2)
    return pl.pallas_call(
        own_kernel,
        grid=(width // QUAD,),
        in_specs=[fixed(top.shape), fixed(bottom.shape)] + q_specs + k_specs + v_specs,
        out_specs=[
            pl.BlockSpec((2 * HALF, QUAD), lambda g: (0, g)),
            pl.BlockSpec((2, 2 * HALF, QUAD), lambda g: (g, 0, 0)),
        ],
        out_shape=[
            jax.ShapeDtypeStruct((2 * HALF, width), BF),
            jax.ShapeDtypeStruct((width // PAIR, 2 * HALF, QUAD), F32),
        ],
        compiler_params=params(),
        cost_estimate=attention_cost(384, 3 * 512),
        name="own",
    )(top, bottom, *q, *k, *v)


def attend_step(modes, valid, a, b, weights, query, total):
    width = a.shape[1]
    k, k_specs = weight_specs(weights, 1)
    v, v_specs = weight_specs(weights, 2)
    return pl.pallas_call(
        functools.partial(step_kernel, modes),
        grid=(width // QUAD,),
        in_specs=[pl.BlockSpec(memory_space=pltpu.SMEM), fixed(a.shape), fixed(b.shape)]
        + k_specs
        + v_specs
        + [
            pl.BlockSpec((2 * HALF, QUAD), lambda g: (0, g)),
            pl.BlockSpec((2, 2 * HALF, QUAD), lambda g: (g, 0, 0)),
        ],
        out_specs=pl.BlockSpec((2, 2 * HALF, QUAD), lambda g: (g, 0, 0)),
        out_shape=jax.ShapeDtypeStruct(total.shape, F32),
        compiler_params=params(),
        cost_estimate=attention_cost(512, 2 * 512),
        name="step",
    )(valid, a, b, *k, *v, query, total)


def attend_last(modes, valid, order, a, b, weights, query, total):
    width = a.shape[1]
    k, k_specs = weight_specs(weights, 1)
    v, v_specs = weight_specs(weights, 2)
    o = [part[3][0] for part in weights]
    o_specs = [
        pl.BlockSpec((PAIR, width), functools.partial(lambda row, g: (row, 0), part[3][1])) for part in weights
    ]
    return pl.pallas_call(
        functools.partial(last_kernel, modes),
        grid=(width // QUAD,),
        in_specs=[pl.BlockSpec(memory_space=pltpu.SMEM)] * 2
        + [fixed(a.shape), fixed(b.shape)]
        + k_specs
        + v_specs
        + o_specs
        + [
            pl.BlockSpec((2 * HALF, QUAD), lambda g: (0, g)),
            pl.BlockSpec((2, 2 * HALF, QUAD), lambda g: (g, 0, 0)),
        ],
        out_specs=fixed((2 * HALF, width)),
        out_shape=jax.ShapeDtypeStruct((2 * HALF, width), BF),
        scratch_shapes=[pltpu.VMEM((width // PAIR, 2 * HALF, PAIR), BF)],
        compiler_params=params(),
        cost_estimate=attention_cost(512, 3 * 512),
        name="last",
    )(valid, order, a, b, *k, *v, *o, query, total)


def along_seq(block, distance):
    count = lax.axis_size("seq")
    return lax.ppermute(block, "seq", [(i, (i + distance) % count) for i in range(count)])


def along_y(block, distance):
    count = lax.axis_size("fsdp")
    return lax.ppermute(block, "fsdp", [(i, (i + 2 * distance) % count) for i in range(count)])


def other_core(block):
    return lax.ppermute(block, "fsdp", [(i, i ^ 1) for i in range(lax.axis_size("fsdp"))])


def gather_weights(w_query, w_key, w_value, w_out):
    own = jnp.concatenate([w_query, w_key, w_value, w_out], axis=0)
    rows = w_query.shape[0]
    below, above = along_y(own, 1), along_y(own, -1)
    other = other_core(own)
    far_qk = along_y(below[: 2 * rows], 1)
    far_vo = along_y(above[2 * rows :], -1)
    other_below, other_above = other_core(below), other_core(above)
    other_far_qk, other_far_vo = other_core(far_qk), other_core(far_vo)
    parts = [tuple((part, i) for i in range(4)) for part in (own, other, below, other_below, above, other_above)]
    for qk, vo in ((far_qk, far_vo), (other_far_qk, other_far_vo)):
        parts.append(((qk, 0), (qk, 1), (vo, 0), (vo, 1)))
    return parts


def weight_order():
    me = lax.axis_index("fsdp")
    y, core = me // 2, me % 2
    return jnp.stack(
        [2 * ((y + dy) % 4) + (core + other) % 2 for dy in (0, 3, 1, 2) for other in (0, 1)]
    ).astype(jnp.int32)


def local(byte_states, group_states, boundaries, w_query, w_key, w_value, w_out):
    own_bytes, own_groups, starts = byte_states[0], group_states[0], boundaries[0]
    rows, width = own_bytes.shape
    owned = own_groups.shape[0]
    position = lax.axis_index("seq")
    order = weight_order()

    carried = along_seq(own_groups[owned - TAIL :], 1)
    weights = gather_weights(w_query, w_key, w_value, w_out)

    far = jnp.int32(2**30)
    padded = jnp.concatenate([jnp.zeros((TAIL,), jnp.int32), starts, jnp.full((1,), far, jnp.int32)])
    window = lax.dynamic_slice_in_dim(padded, position * owned, owned + TAIL + 1, 0) - position * rows
    begin, end = window[:-1], window[1:]
    gap = jnp.full((PAIR - TAIL,), far, jnp.int32)
    window = jnp.stack([jnp.concatenate([w[:TAIL], gap, w[TAIL:]]) for w in (begin, end)])

    out_bottom, bottom = prep(HALF, order, window, own_bytes, carried, own_groups)
    down = along_seq(bottom, 4)
    out_top, top = prep(0, order, window, own_bytes, carried, own_groups)
    up = along_seq(top, 1)
    dechunked = jnp.concatenate([out_top, out_bottom], axis=0)

    query, total = attend_own(top, bottom, weights)

    full = ("full", "full")
    for k in range(1, 5):
        valid = jnp.stack([position >= k, position >= 5 - k]).astype(jnp.int32)
        modes = (full if k < 4 else ("from", "none"), full if k > 1 else ("full", "from"))
        if k < 4:
            total = attend_step(modes, valid, up, down, weights, query, total)
            up, down = along_seq(up, 1), along_seq(down, -1)
        else:
            attended = attend_last(modes, valid, order, up, down, weights, query, total)
    return dechunked[None], attended[None]


def solution(mesh):
    placed = (P("fsdp", "seq", None),) * 2 + (P("fsdp", None),) * 5
    return jax.shard_map(
        local,
        mesh=mesh,
        in_specs=placed,
        out_specs=(P("fsdp", "seq", None), P("fsdp", "seq", None)),
        check_vma=False,
    )
```

```python
import functools

import jax
import jax.numpy as jnp
from jax import lax
from jax.experimental import pallas as pl
from jax.experimental.pallas import tpu as pltpu
from jax.sharding import PartitionSpec as P

HEAD_DIM = 64
TAIL = 64
PAIR = 2 * HEAD_DIM
QUAD = 2 * PAIR
HALF = 256
UPPER = 256
BLOCK = 512
EPS = 1e-6
QUERY_FACTOR = 16.0 / HEAD_DIM * 1.4426950408889634
BF = jnp.bfloat16
F32 = jnp.float32
VMEM_WHOLE = pl.BlockSpec(memory_space=pltpu.VMEM)
SMEM_WHOLE = pl.BlockSpec(memory_space=pltpu.SMEM)
SMALL = pl.CostEstimate(flops=1, bytes_accessed=1, transcendentals=0)
TOKEN = jax.ShapeDtypeStruct((8, 128), F32)
NT = (((1,), (1,)), ((), ()))
VMEM_LIMIT = 60 * 2**20


def params():
    return pltpu.CompilerParams(vmem_limit_bytes=VMEM_LIMIT)


def prep_kernel(order_ref, win_ref, bytes_ref, carried_ref, groups_ref, out_ref, upper_ref, lower_ref, hold):
    rows, width = bytes_ref.shape
    start, following = win_ref[0:1, :], win_ref[1:2, :]

    def one_hot(lo, hi):
        position = lax.broadcasted_iota(jnp.int32, (rows, hi - lo), 0)
        return ((start[:, lo:hi] <= position) & (following[:, lo:hi] > position)).astype(F32).astype(BF)

    own = groups_ref.shape[0]
    lifted = jnp.dot(one_hot(PAIR, PAIR + own), groups_ref[...], preferred_element_type=F32)
    lifted += jnp.dot(one_hot(0, TAIL), carried_ref[...], preferred_element_type=F32)
    dechunked = (bytes_ref[...].astype(F32) + lifted).astype(BF)
    out_ref[...] = dechunked
    wide = dechunked.astype(F32)
    mean = jnp.sum(wide * wide, axis=-1, keepdims=True) * (1.0 / width)
    hold[...] = (wide * lax.rsqrt(mean + EPS)).astype(BF)
    for r in range(width // PAIR):
        at = pl.multiple_of(order_ref[r] * PAIR, PAIR)
        upper_ref[:, r * PAIR : (r + 1) * PAIR] = hold[:UPPER, pl.ds(at, PAIR)]
        lower_ref[:, r * PAIR : (r + 1) * PAIR] = hold[UPPER:, pl.ds(at, PAIR)]


def whole(shape):
    return pl.BlockSpec(shape, lambda *_: (0,) * len(shape))


def prep(order, window, own_bytes, carried, own_groups):
    rows, width = own_bytes.shape
    shapes = [(rows, width), (UPPER, width), (rows - UPPER, width)]
    return pl.pallas_call(
        prep_kernel,
        grid=(1,),
        in_specs=[SMEM_WHOLE] + [whole(x.shape) for x in (window, own_bytes, carried, own_groups)],
        out_specs=[whole(shape) for shape in shapes],
        out_shape=[jax.ShapeDtypeStruct(shape, BF) for shape in shapes],
        scratch_shapes=[pltpu.VMEM((rows, width), BF)],
        compiler_params=params(),
        cost_estimate=SMALL,
        name="prep",
    )(order, window, own_bytes, carried, own_groups)


def stack_kernel(*refs):
    out_ref = refs[-1]
    rows = refs[0].shape[0]
    for i, ref in enumerate(refs[:-1]):
        out_ref[i * rows : (i + 1) * rows] = ref[...]


def stack(*arrays):
    rows, width = arrays[0].shape
    shape = (len(arrays) * rows, width)
    return pl.pallas_call(
        stack_kernel,
        grid=(1,),
        in_specs=[whole((rows, width))] * len(arrays),
        out_specs=whole(shape),
        out_shape=jax.ShapeDtypeStruct(shape, BF),
        compiler_params=params(),
        cost_estimate=SMALL,
        name="stack",
    )(*arrays)


def head_norm(raw, factor):
    n = raw.shape[1]
    row = lax.broadcasted_iota(jnp.int32, (n, n), 0) // HEAD_DIM
    column = lax.broadcasted_iota(jnp.int32, (n, n), 1) // HEAD_DIM
    mean_of_head = jnp.where(row == column, 1.0 / HEAD_DIM, 0.0).astype(BF)
    mean_square = jnp.dot((raw * raw).astype(BF), mean_of_head, preferred_element_type=F32)
    return (raw * (lax.rsqrt(mean_square + EPS) * factor)).astype(BF)


def project(x, weight):
    return jnp.dot(x, weight, preferred_element_type=F32)


def joined(refs):
    return jnp.concatenate([r[...] for r in refs], axis=0)


def weights_of(scores, keep):
    weights = jnp.exp2(scores)
    if keep is not None:
        weights = jnp.where(keep, weights, 0.0)
    return weights.astype(BF)


def attend_quad(query, key, value, ones, plan, put):
    low = lax.broadcasted_iota(jnp.int32, ones.shape, 1) < HEAD_DIM
    low_q = low[:HALF]
    zero = jnp.zeros(ones.shape, BF)
    zero_q = zero[:HALF]
    for pair in range(2):
        lanes = slice(pair * PAIR, (pair + 1) * PAIR)
        k, v = key[:, lanes], value[:, lanes]
        right_a = jnp.concatenate([jnp.where(low, v, zero), jnp.where(low, ones, zero)], axis=1)
        right_b = jnp.concatenate([jnp.where(low, zero, v), jnp.where(low, zero, ones)], axis=1)
        for part in range(2):
            rows = slice(part * HALF, (part + 1) * HALF)
            q = query[rows, lanes]
            left, right = [], []
            for begin, end, rule in plan[part]:
                keep = None
                if rule is not None:
                    shape = (HALF, end - begin)
                    i = part * HALF + lax.broadcasted_iota(jnp.int32, shape, 0)
                    keep = rule(i, begin + lax.broadcasted_iota(jnp.int32, shape, 1))
                for q_head, v_head in (
                    (jnp.where(low_q, q, zero_q), right_a),
                    (jnp.where(low_q, zero_q, q), right_b),
                ):
                    scores = lax.dot_general(q_head, k[begin:end], NT, preferred_element_type=F32)
                    left.append(weights_of(scores, keep))
                    right.append(v_head[begin:end])
            total = jnp.dot(
                jnp.concatenate(left, axis=1), jnp.concatenate(right, axis=0), preferred_element_type=F32
            )
            put(pair, rows, total)


def until(i, j):
    return j <= i


def since(i, j):
    return j >= i


FIRST_PLAN = (
    ((0, HALF, until), (BLOCK, BLOCK + UPPER, None)),
    ((0, HALF, None), (HALF, BLOCK, until), (BLOCK, BLOCK + UPPER, None)),
)
SECOND_PLAN = (
    ((0, BLOCK, None),),
    ((0, UPPER, None), (UPPER, BLOCK, since)),
)
FULL_PLAN = (((0, BLOCK, None),),) * 2
LAST_PLAN = (
    ((0, UPPER, since), (UPPER, 3 * HALF, None)),
    ((UPPER, 3 * HALF, None),),
)


def keys_of(x, w_k, w_v, valid_ref, valid):
    key = head_norm(project(x, joined(w_k)), 1.0)
    value = project(x, joined(w_v))
    values, ones = [], []
    for n, place in enumerate(valid):
        part, one = value[n * HALF : (n + 1) * HALF], jnp.ones((HALF, PAIR), F32)
        if place is not None:
            counts = valid_ref[place] > 0
            part, one = jnp.where(counts, part, 0.0), jnp.where(counts, one, 0.0)
        values.append(part.astype(BF))
        ones.append(one.astype(BF))
    return key, jnp.concatenate(values, axis=0), jnp.concatenate(ones, axis=0)


def first_kernel(*refs):
    valid_ref = refs[0]
    w_q, w_k, w_v = refs[4:12], refs[12:20], refs[20:28]
    query_ref, total_ref, token_ref = refs[28:]
    token_ref[...] = jnp.zeros_like(token_ref)
    x = joined(refs[1:4])
    query = head_norm(project(x[:BLOCK], joined(w_q)), QUERY_FACTOR)
    query_ref[...] = query

    def put(pair, rows, total):
        total_ref[pair, rows, :] = total

    attend_quad(query, *keys_of(x, w_k, w_v, valid_ref, (None, None, 0)), FIRST_PLAN, put)


def step_kernel(plan, valid, *refs):
    n = len(valid)
    valid_ref, rows = refs[0], refs[1 : 1 + n]
    w_k, w_v = refs[1 + n : 9 + n], refs[9 + n : 17 + n]
    query_ref, total_ref, _, out_ref, token_ref = refs[17 + n :]
    token_ref[...] = jnp.zeros_like(token_ref)

    def put(pair, rows, total):
        out_ref[pair, rows, :] = total_ref[pair, rows, :] + total

    attend_quad(query_ref[...], *keys_of(joined(rows), w_k, w_v, valid_ref, valid), plan, put)


def last_kernel(plan, valid, *refs):
    n = len(valid)
    valid_ref, order_ref, rows = refs[0], refs[1], refs[2 : 2 + n]
    w_k, w_v, w_out = refs[2 + n : 10 + n], refs[10 + n : 18 + n], refs[18 + n : 20 + n]
    query_ref, total_ref, _, out_ref, context = refs[20 + n :]
    g = pl.program_id(0)

    def put(pair, rows, total):
        total = total_ref[pair, rows, :] + total
        context[2 * g + pair, rows, :] = (total[:, :PAIR] / total[:, PAIR:]).astype(BF)

    attend_quad(query_ref[...], *keys_of(joined(rows), w_k, w_v, valid_ref, valid), plan, put)

    @pl.when(g == pl.num_programs(0) - 1)
    def _():
        x = jnp.concatenate([context[order_ref[r]] for r in (0, 2, 4, 6, 1, 3, 5, 7)], axis=1)
        out_ref[...] = project(x, joined(w_out)).astype(BF)


def weight_specs(parts, kind):
    return [pl.BlockSpec((PAIR, QUAD), lambda g: (kind, g))] * len(parts)


QUERY_SPEC = pl.BlockSpec((BLOCK, QUAD), lambda g: (0, g))
TOTAL_SPEC = pl.BlockSpec((2, BLOCK, QUAD), lambda g: (g, 0, 0))


def attend_first(valid, rows, parts):
    width = rows[0].shape[1]
    return pl.pallas_call(
        first_kernel,
        grid=(width // QUAD,),
        in_specs=[SMEM_WHOLE]
        + [whole(x.shape) for x in rows]
        + weight_specs(parts, 0)
        + weight_specs(parts, 1)
        + weight_specs(parts, 2),
        out_specs=[QUERY_SPEC, TOTAL_SPEC, whole(TOKEN.shape)],
        out_shape=[
            jax.ShapeDtypeStruct((BLOCK, width), BF),
            jax.ShapeDtypeStruct((width // PAIR, BLOCK, QUAD), F32),
            TOKEN,
        ],
        compiler_params=params(),
        cost_estimate=SMALL,
        name="first",
    )(valid, *rows, *parts, *parts, *parts)


def attend_step(plan, places, valid, rows, parts, query, total, token):
    width = rows[0].shape[1]
    return pl.pallas_call(
        functools.partial(step_kernel, plan, places),
        grid=(width // QUAD,),
        in_specs=[SMEM_WHOLE]
        + [whole(x.shape) for x in rows]
        + weight_specs(parts, 1)
        + weight_specs(parts, 2)
        + [QUERY_SPEC, TOTAL_SPEC, pl.BlockSpec(memory_space=pl.ANY)],
        out_specs=[TOTAL_SPEC, whole(TOKEN.shape)],
        out_shape=[jax.ShapeDtypeStruct(total.shape, F32), TOKEN],
        compiler_params=params(),
        cost_estimate=SMALL,
        name="step",
    )(valid, *rows, *parts, *parts, query, total, token)


def attend_last(plan, places, valid, order, rows, parts, w_out, query, total, token):
    width = rows[0].shape[1]
    return pl.pallas_call(
        functools.partial(last_kernel, plan, places),
        grid=(width // QUAD,),
        in_specs=[SMEM_WHOLE] * 2
        + [whole(x.shape) for x in rows]
        + weight_specs(parts, 1)
        + weight_specs(parts, 2)
        + [whole(w.shape) for w in w_out]
        + [QUERY_SPEC, TOTAL_SPEC, pl.BlockSpec(memory_space=pl.ANY)],
        out_specs=whole((BLOCK, width)),
        out_shape=jax.ShapeDtypeStruct((BLOCK, width), BF),
        scratch_shapes=[pltpu.VMEM((width // PAIR, BLOCK, PAIR), BF)],
        compiler_params=params(),
        cost_estimate=SMALL,
        name="last",
    )(valid, order, *rows, *parts, *parts, *w_out, query, total, token)


def along_seq(block, distance):
    count = lax.axis_size("seq")
    return lax.ppermute(block, "seq", [(i, (i + distance) % count) for i in range(count)])


def over_fsdp(block, dy, other):
    count = lax.axis_size("fsdp")
    return lax.ppermute(block, "fsdp", [(i, (i // 2 * 2 + 2 * dy) % count + (i + other) % 2) for i in range(count)])


def together(*arrays):
    return lax.optimization_barrier(arrays)


def gather_parts(rows):
    return [rows] + [over_fsdp(rows, dy, 0) for dy in (1, -1, 2)]


def weight_order():
    me = lax.axis_index("fsdp")
    y, core = me // 2, me % 2
    return jnp.stack(
        [2 * ((y + dy) % 4) + (core + other) % 2 for dy in (0, 3, 1, 2) for other in (0, 1)]
    ).astype(jnp.int32)


def local(byte_states, group_states, boundaries, w_query, w_key, w_value, w_out):
    own_bytes, own_groups, starts = byte_states[0], group_states[0], boundaries[0]
    rows, width = own_bytes.shape
    owned = own_groups.shape[0]
    position = lax.axis_index("seq")
    order = weight_order()
    valid = jnp.stack([position >= k for k in range(1, 5)]).astype(jnp.int32)

    tail, w_query, w_key, w_value = together(own_groups[owned - TAIL :], w_query, w_key, w_value)
    carried = along_seq(tail, 1)
    packed = stack(w_query, w_key, w_value)
    own_core = gather_parts(packed)

    far = jnp.int32(2**30)
    padded = jnp.concatenate([jnp.zeros((TAIL,), jnp.int32), starts, jnp.full((1,), far, jnp.int32)])
    window = lax.dynamic_slice_in_dim(padded, position * owned, owned + TAIL + 1, 0) - position * rows
    begin, end = window[:-1], window[1:]
    gap = jnp.full((PAIR - TAIL,), far, jnp.int32)
    window = jnp.stack([jnp.concatenate([w[:TAIL], gap, w[TAIL:]]) for w in (begin, end)])

    dechunked, upper, lower = prep(order, window, own_bytes, carried, own_groups)

    up, down = {1: along_seq(upper, 1)}, {4: along_seq(lower, 4)}
    other = [over_fsdp(part, 0, 1) for part in own_core[:3]]
    own_core[3], up[1], down[4] = together(own_core[3], up[1], down[4])
    other.append(over_fsdp(own_core[3], 0, 1))

    other[3], w_out = together(other[3], w_out)
    w_out_core = gather_parts(w_out)
    up[2], down[3] = along_seq(up[1], 1), along_seq(down[4], -1)
    parts = [part for pair in zip(own_core, other) for part in pair]
    query, total, token = attend_first(valid, (upper, lower, up[1]), parts)

    up[2], down[3], token, *w_out_core = together(up[2], down[3], token, *w_out_core)
    up[3], down[2] = along_seq(up[2], 1), along_seq(down[3], -1)
    token, w_out_core = together(token, stack(*w_out_core))
    w_out = w_out_core, over_fsdp(w_out_core, 0, 1)
    rows = (up[2], down[4])
    total, token = attend_step(SECOND_PLAN, (1, 3), valid, rows, parts, query, total, token)

    up[3], down[2], token = together(up[3], down[2], token)
    up[4], down[1] = along_seq(up[3], 1), along_seq(down[2], -1)
    rows = (up[3], down[3])
    total, token = attend_step(FULL_PLAN, (2, 2), valid, rows, parts, query, total, token)

    rows = (up[4], down[2], down[1])
    attended = attend_last(LAST_PLAN, (3, 1, 0), valid, order, rows, parts, w_out, query, total, token)
    return dechunked[None], attended[None]


def solution(mesh):
    placed = (P("fsdp", "seq", None),) * 2 + (P("fsdp", None),) * 5
    return jax.shard_map(
        local,
        mesh=mesh,
        in_specs=placed,
        out_specs=(P("fsdp", "seq", None), P("fsdp", "seq", None)),
        check_vma=False,
    )
```

```python
import functools

import jax
import jax.numpy as jnp
from jax import lax
from jax.experimental import pallas as pl
from jax.experimental.pallas import tpu as pltpu
from jax.sharding import PartitionSpec as P

HEAD_DIM = 64
TAIL = 64
PAIR = 2 * HEAD_DIM
QUAD = 2 * PAIR
HALF = 256
UPPER = 384
BLOCK = 512
EPS = 1e-6
QUERY_FACTOR = 16.0 / HEAD_DIM * 1.4426950408889634
BF = jnp.bfloat16
F32 = jnp.float32
VMEM_WHOLE = pl.BlockSpec(memory_space=pltpu.VMEM)
SMEM_WHOLE = pl.BlockSpec(memory_space=pltpu.SMEM)
SMALL = pl.CostEstimate(flops=1, bytes_accessed=1, transcendentals=0)
TOKEN = jax.ShapeDtypeStruct((8, 128), F32)
NT = (((1,), (1,)), ((), ()))
VMEM_LIMIT = 60 * 2**20


def params():
    return pltpu.CompilerParams(vmem_limit_bytes=VMEM_LIMIT)


def prep_kernel(order_ref, win_ref, bytes_ref, carried_ref, groups_ref, out_ref, upper_ref, lower_ref, hold):
    rows, width = bytes_ref.shape
    start, following = win_ref[0:1, :], win_ref[1:2, :]

    def one_hot(lo, hi):
        position = lax.broadcasted_iota(jnp.int32, (rows, hi - lo), 0)
        return ((start[:, lo:hi] <= position) & (following[:, lo:hi] > position)).astype(F32).astype(BF)

    own = groups_ref.shape[0]
    lifted = jnp.dot(one_hot(PAIR, PAIR + own), groups_ref[...], preferred_element_type=F32)
    lifted += jnp.dot(one_hot(0, TAIL), carried_ref[...], preferred_element_type=F32)
    dechunked = (bytes_ref[...].astype(F32) + lifted).astype(BF)
    out_ref[...] = dechunked
    wide = dechunked.astype(F32)
    mean = jnp.sum(wide * wide, axis=-1, keepdims=True) * (1.0 / width)
    hold[...] = (wide * lax.rsqrt(mean + EPS)).astype(BF)
    for r in range(width // PAIR):
        at = pl.multiple_of(order_ref[r] * PAIR, PAIR)
        upper_ref[:, r * PAIR : (r + 1) * PAIR] = hold[:UPPER, pl.ds(at, PAIR)]
        lower_ref[:, r * PAIR : (r + 1) * PAIR] = hold[UPPER:, pl.ds(at, PAIR)]


def whole(shape):
    return pl.BlockSpec(shape, lambda *_: (0,) * len(shape))


def prep(order, window, own_bytes, carried, own_groups):
    rows, width = own_bytes.shape
    shapes = [(rows, width), (UPPER, width), (rows - UPPER, width)]
    return pl.pallas_call(
        prep_kernel,
        grid=(1,),
        in_specs=[SMEM_WHOLE] + [whole(x.shape) for x in (window, own_bytes, carried, own_groups)],
        out_specs=[whole(shape) for shape in shapes],
        out_shape=[jax.ShapeDtypeStruct(shape, BF) for shape in shapes],
        scratch_shapes=[pltpu.VMEM((rows, width), BF)],
        compiler_params=params(),
        cost_estimate=SMALL,
        name="prep",
    )(order, window, own_bytes, carried, own_groups)


def stack_kernel(*refs):
    out_ref = refs[-1]
    rows = refs[0].shape[0]
    for i, ref in enumerate(refs[:-1]):
        out_ref[i * rows : (i + 1) * rows] = ref[...]


def stack(*arrays):
    rows, width = arrays[0].shape
    shape = (len(arrays) * rows, width)
    return pl.pallas_call(
        stack_kernel,
        grid=(1,),
        in_specs=[whole((rows, width))] * len(arrays),
        out_specs=whole(shape),
        out_shape=jax.ShapeDtypeStruct(shape, BF),
        compiler_params=params(),
        cost_estimate=SMALL,
        name="stack",
    )(*arrays)


def head_norm(raw, factor):
    n = raw.shape[1]
    row = lax.broadcasted_iota(jnp.int32, (n, n), 0) // HEAD_DIM
    column = lax.broadcasted_iota(jnp.int32, (n, n), 1) // HEAD_DIM
    mean_of_head = jnp.where(row == column, 1.0 / HEAD_DIM, 0.0).astype(BF)
    mean_square = jnp.dot((raw * raw).astype(BF), mean_of_head, preferred_element_type=F32)
    return (raw * (lax.rsqrt(mean_square + EPS) * factor)).astype(BF)


def project(x, weight):
    return jnp.dot(x, weight, preferred_element_type=F32)


def joined(refs):
    return jnp.concatenate([r[...] for r in refs], axis=0)


def weights_of(scores, keep):
    weights = jnp.exp2(scores)
    if keep is not None:
        weights = jnp.where(keep, weights, 0.0)
    return weights.astype(BF)


def attend_quad(query, key, value, ones, plan, put):
    low = lax.broadcasted_iota(jnp.int32, ones.shape, 1) < HEAD_DIM
    low_q = low[:HALF]
    zero = jnp.zeros(ones.shape, BF)
    zero_q = zero[:HALF]
    for pair in range(2):
        lanes = slice(pair * PAIR, (pair + 1) * PAIR)
        k, v = key[:, lanes], value[:, lanes]
        right_a = jnp.concatenate([jnp.where(low, v, zero), jnp.where(low, ones, zero)], axis=1)
        right_b = jnp.concatenate([jnp.where(low, zero, v), jnp.where(low, zero, ones)], axis=1)
        for part in range(2):
            rows = slice(part * HALF, (part + 1) * HALF)
            q = query[rows, lanes]
            left, right = [], []
            for begin, end, rule in plan[part]:
                keep = None
                if rule is not None:
                    shape = (HALF, end - begin)
                    i = part * HALF + lax.broadcasted_iota(jnp.int32, shape, 0)
                    keep = rule(i, begin + lax.broadcasted_iota(jnp.int32, shape, 1))
                for q_head, v_head in (
                    (jnp.where(low_q, q, zero_q), right_a),
                    (jnp.where(low_q, zero_q, q), right_b),
                ):
                    scores = lax.dot_general(q_head, k[begin:end], NT, preferred_element_type=F32)
                    left.append(weights_of(scores, keep))
                    right.append(v_head[begin:end])
            total = jnp.dot(
                jnp.concatenate(left, axis=1), jnp.concatenate(right, axis=0), preferred_element_type=F32
            )
            put(pair, rows, total)


def until(i, j):
    return j <= i


def upper_since(i, j):
    return (j >= UPPER) | (j >= i)


def first_lower_since(i, j):
    return (j < BLOCK + UPPER) | (j - BLOCK >= i)


FIRST_PLAN = (
    ((0, HALF, until), (BLOCK, 2 * BLOCK, None)),
    ((0, HALF, None), (HALF, BLOCK, until), (BLOCK, 2 * BLOCK, first_lower_since)),
)
FIRST_PLACES = (None, None, 0, 3)
FULL_PLAN = (((0, BLOCK, None),),) * 2
LAST_PLAN = (((0, BLOCK, upper_since),), ((HALF, BLOCK, upper_since),))


def keys_of(refs, w_k, w_v, valid_ref, valid):
    x = joined(refs)
    key = head_norm(project(x, joined(w_k)), 1.0)
    value = project(x, joined(w_v))
    values, ones, row = [], [], 0
    for ref, place in zip(refs, valid):
        rows = ref.shape[0]
        part, one = value[row : row + rows], jnp.ones((rows, PAIR), F32)
        if place is not None:
            counts = valid_ref[place] > 0
            part, one = jnp.where(counts, part, 0.0), jnp.where(counts, one, 0.0)
        values.append(part.astype(BF))
        ones.append(one.astype(BF))
        row += rows
    return key, jnp.concatenate(values, axis=0), jnp.concatenate(ones, axis=0)


def first_kernel(*refs):
    n = len(FIRST_PLACES)
    valid_ref, rows = refs[0], refs[1 : 1 + n]
    w_q, w_k, w_v = refs[1 + n : 9 + n], refs[9 + n : 17 + n], refs[17 + n : 25 + n]
    query_ref, total_ref, token_ref = refs[25 + n :]
    token_ref[...] = jnp.zeros_like(token_ref)
    query = head_norm(project(joined(rows[:2]), joined(w_q)), QUERY_FACTOR)
    query_ref[...] = query

    def put(pair, rows, total):
        total_ref[pair, rows, :] = total

    attend_quad(query, *keys_of(rows, w_k, w_v, valid_ref, FIRST_PLACES), FIRST_PLAN, put)


def step_kernel(plan, valid, *refs):
    n = len(valid)
    valid_ref, rows = refs[0], refs[1 : 1 + n]
    w_k, w_v = refs[1 + n : 9 + n], refs[9 + n : 17 + n]
    query_ref, total_ref, _, out_ref, token_ref = refs[17 + n :]
    token_ref[...] = jnp.zeros_like(token_ref)

    def put(pair, rows, total):
        out_ref[pair, rows, :] = total_ref[pair, rows, :] + total

    attend_quad(query_ref[...], *keys_of(rows, w_k, w_v, valid_ref, valid), plan, put)


def last_kernel(plan, valid, *refs):
    n = len(valid)
    valid_ref, order_ref, rows = refs[0], refs[1], refs[2 : 2 + n]
    w_k, w_v, w_out = refs[2 + n : 10 + n], refs[10 + n : 18 + n], refs[18 + n : 26 + n]
    query_ref, total_ref, _, out_ref, context = refs[26 + n :]
    g = pl.program_id(0)

    def put(pair, rows, total):
        total = total_ref[pair, rows, :] + total
        context[2 * g + pair, rows, :] = (total[:, :PAIR] / total[:, PAIR:]).astype(BF)

    attend_quad(query_ref[...], *keys_of(rows, w_k, w_v, valid_ref, valid), plan, put)

    @pl.when(g == pl.num_programs(0) - 1)
    def _():
        x = jnp.concatenate([context[order_ref[r]] for r in range(8)], axis=1)
        out_ref[...] = project(x, joined(w_out)).astype(BF)


def weight_arrays(parts, kind):
    return [part[kind][0] for part in parts]


def weight_specs(parts, kind):
    return [pl.BlockSpec((PAIR, QUAD), functools.partial(lambda row, g: (row, g), part[kind][1])) for part in parts]


QUERY_SPEC = pl.BlockSpec((BLOCK, QUAD), lambda g: (0, g))
TOTAL_SPEC = pl.BlockSpec((2, BLOCK, QUAD), lambda g: (g, 0, 0))


def attend_first(valid, rows, parts):
    width = rows[0].shape[1]
    return pl.pallas_call(
        first_kernel,
        grid=(width // QUAD,),
        in_specs=[SMEM_WHOLE]
        + [whole(x.shape) for x in rows]
        + weight_specs(parts, 0)
        + weight_specs(parts, 1)
        + weight_specs(parts, 2),
        out_specs=[QUERY_SPEC, TOTAL_SPEC, whole(TOKEN.shape)],
        out_shape=[
            jax.ShapeDtypeStruct((BLOCK, width), BF),
            jax.ShapeDtypeStruct((width // PAIR, BLOCK, QUAD), F32),
            TOKEN,
        ],
        compiler_params=params(),
        cost_estimate=SMALL,
        name="first",
    )(valid, *rows, *(w for kind in range(3) for w in weight_arrays(parts, kind)))


def attend_step(plan, places, valid, rows, parts, query, total, token):
    width = rows[0].shape[1]
    return pl.pallas_call(
        functools.partial(step_kernel, plan, places),
        grid=(width // QUAD,),
        in_specs=[SMEM_WHOLE]
        + [whole(x.shape) for x in rows]
        + weight_specs(parts, 1)
        + weight_specs(parts, 2)
        + [QUERY_SPEC, TOTAL_SPEC, pl.BlockSpec(memory_space=pl.ANY)],
        out_specs=[TOTAL_SPEC, whole(TOKEN.shape)],
        out_shape=[jax.ShapeDtypeStruct(total.shape, F32), TOKEN],
        compiler_params=params(),
        cost_estimate=SMALL,
        name="step",
    )(valid, *rows, *weight_arrays(parts, 1), *weight_arrays(parts, 2), query, total, token)


def attend_last(plan, places, valid, order, rows, parts, query, total, token):
    width = rows[0].shape[1]
    return pl.pallas_call(
        functools.partial(last_kernel, plan, places),
        grid=(width // QUAD,),
        in_specs=[SMEM_WHOLE] * 2
        + [whole(x.shape) for x in rows]
        + weight_specs(parts, 1)
        + weight_specs(parts, 2)
        + [
            pl.BlockSpec((PAIR, width), functools.partial(lambda row, g: (row, 0), part[3][1])) for part in parts
        ]
        + [QUERY_SPEC, TOTAL_SPEC, pl.BlockSpec(memory_space=pl.ANY)],
        out_specs=whole((BLOCK, width)),
        out_shape=jax.ShapeDtypeStruct((BLOCK, width), BF),
        scratch_shapes=[pltpu.VMEM((width // PAIR, BLOCK, PAIR), BF)],
        compiler_params=params(),
        cost_estimate=SMALL,
        name="last",
    )(valid, order, *rows, *(w for kind in (1, 2, 3) for w in weight_arrays(parts, kind)), query, total, token)


def along_seq(block, distance):
    count = lax.axis_size("seq")
    return lax.ppermute(block, "seq", [(i, (i + distance) % count) for i in range(count)])


def over_fsdp(block, dy, other):
    count = lax.axis_size("fsdp")
    return lax.ppermute(block, "fsdp", [(i, (i // 2 * 2 + 2 * dy) % count + (i + other) % 2) for i in range(count)])


def together(*arrays):
    return lax.optimization_barrier(arrays)


def weight_order():
    me = lax.axis_index("fsdp")
    y, core = me // 2, me % 2
    return jnp.stack(
        [2 * ((y + dy) % 4) + (core + other) % 2 for dy in (0, 3, 1, 2) for other in (0, 1)]
    ).astype(jnp.int32)


def local(byte_states, group_states, boundaries, w_query, w_key, w_value, w_out):
    own_bytes, own_groups, starts = byte_states[0], group_states[0], boundaries[0]
    rows, width = own_bytes.shape
    owned = own_groups.shape[0]
    position = lax.axis_index("seq")
    order = weight_order()
    valid = jnp.stack([position >= k for k in range(1, 5)]).astype(jnp.int32)

    tail, *own_weights = together(own_groups[owned - TAIL :], w_query, w_key, w_value, w_out)
    carried = along_seq(tail, 1)
    packed = stack(*own_weights)
    half = packed.shape[0] // 2
    below, above = over_fsdp(packed, 1, 0), over_fsdp(packed, -1, 0)
    far = over_fsdp(below[:half], 1, 0), over_fsdp(above[half:], -1, 0)

    never = jnp.int32(2**30)
    padded = jnp.concatenate([jnp.zeros((TAIL,), jnp.int32), starts, jnp.full((1,), never, jnp.int32)])
    window = lax.dynamic_slice_in_dim(padded, position * owned, owned + TAIL + 1, 0) - position * rows
    begin, end = window[:-1], window[1:]
    gap = jnp.full((PAIR - TAIL,), never, jnp.int32)
    window = jnp.stack([jnp.concatenate([w[:TAIL], gap, w[TAIL:]]) for w in (begin, end)])

    dechunked, upper, lower = prep(order, window, own_bytes, carried, own_groups)

    up, down = {1: along_seq(upper, 1)}, {4: along_seq(lower, 4)}
    *far, up[1], down[4] = together(*far, up[1], down[4])
    parts = []
    for part in (packed, below, above):
        parts += [tuple((x, kind) for kind in range(4)) for x in (part, over_fsdp(part, 0, 1))]
    for a, b in (far, [over_fsdp(x, 0, 1) for x in far]):
        parts.append(((a, 0), (a, 1), (b, 0), (b, 1)))

    up[2], down[3] = along_seq(up[1], 1), along_seq(down[4], -1)
    query, total, token = attend_first(valid, (upper, lower, up[1], down[4]), parts)

    up[2], down[3], token = together(up[2], down[3], token)
    up[3], down[2] = along_seq(up[2], 1), along_seq(down[3], -1)
    total, token = attend_step(FULL_PLAN, (1, 2), valid, (up[2], down[3]), parts, query, total, token)

    up[3], down[2], token = together(up[3], down[2], token)
    up[4], down[1] = along_seq(up[3], 1), along_seq(down[2], -1)
    total, token = attend_step(FULL_PLAN, (2, 1), valid, (up[3], down[2]), parts, query, total, token)
    attended = attend_last(LAST_PLAN, (3, 0), valid, order, (up[4], down[1]), parts, query, total, token)
    return dechunked[None], attended[None]


def solution(mesh):
    placed = (P("fsdp", "seq", None),) * 2 + (P("fsdp", None),) * 5
    return jax.shard_map(
        local,
        mesh=mesh,
        in_specs=placed,
        out_specs=(P("fsdp", "seq", None), P("fsdp", "seq", None)),
        check_vma=False,
    )
```

```python
import functools

import jax
import jax.numpy as jnp
from jax import lax
from jax.experimental import pallas as pl
from jax.experimental.pallas import tpu as pltpu
from jax.sharding import PartitionSpec as P

HEAD_DIM = 64
TAIL = 64
PAIR = 2 * HEAD_DIM
QUAD = 2 * PAIR
HALF = 256
UPPER = 384
BLOCK = 512
EPS = 1e-6
QUERY_FACTOR = 16.0 / HEAD_DIM * 1.4426950408889634
BF = jnp.bfloat16
F32 = jnp.float32
VMEM_WHOLE = pl.BlockSpec(memory_space=pltpu.VMEM)
SMEM_WHOLE = pl.BlockSpec(memory_space=pltpu.SMEM)
SMALL = pl.CostEstimate(flops=1, bytes_accessed=1, transcendentals=0)
TOKEN = jax.ShapeDtypeStruct((8, 128), F32)
NT = (((1,), (1,)), ((), ()))
VMEM_LIMIT = 63 * 2**20


def params():
    return pltpu.CompilerParams(vmem_limit_bytes=VMEM_LIMIT)


def prep_kernel(order_ref, win_ref, bytes_ref, carried_ref, groups_ref, out_ref, upper_ref, lower_ref, hold):
    rows, width = bytes_ref.shape
    start, following = win_ref[0:1, :], win_ref[1:2, :]

    def one_hot(lo, hi):
        position = lax.broadcasted_iota(jnp.int32, (rows, hi - lo), 0)
        return ((start[:, lo:hi] <= position) & (following[:, lo:hi] > position)).astype(F32).astype(BF)

    own = groups_ref.shape[0]
    lifted = jnp.dot(one_hot(PAIR, PAIR + own), groups_ref[...], preferred_element_type=F32)
    lifted += jnp.dot(one_hot(0, TAIL), carried_ref[...], preferred_element_type=F32)
    dechunked = (bytes_ref[...].astype(F32) + lifted).astype(BF)
    out_ref[...] = dechunked
    wide = dechunked.astype(F32)
    mean = jnp.sum(wide * wide, axis=-1, keepdims=True) * (1.0 / width)
    hold[...] = (wide * lax.rsqrt(mean + EPS)).astype(BF)
    for r in range(width // PAIR):
        at = pl.multiple_of(order_ref[r] * PAIR, PAIR)
        upper_ref[:, r * PAIR : (r + 1) * PAIR] = hold[:UPPER, pl.ds(at, PAIR)]
        lower_ref[:, r * PAIR : (r + 1) * PAIR] = hold[UPPER:, pl.ds(at, PAIR)]


def whole(shape):
    return pl.BlockSpec(shape, lambda *_: (0,) * len(shape))


def prep(order, window, own_bytes, carried, own_groups):
    rows, width = own_bytes.shape
    shapes = [(rows, width), (UPPER, width), (rows - UPPER, width)]
    return pl.pallas_call(
        prep_kernel,
        grid=(1,),
        in_specs=[SMEM_WHOLE] + [whole(x.shape) for x in (window, own_bytes, carried, own_groups)],
        out_specs=[whole(shape) for shape in shapes],
        out_shape=[jax.ShapeDtypeStruct(shape, BF) for shape in shapes],
        scratch_shapes=[pltpu.VMEM((rows, width), BF)],
        compiler_params=params(),
        cost_estimate=SMALL,
        name="prep",
    )(order, window, own_bytes, carried, own_groups)


def stack_kernel(*refs):
    out_ref = refs[-1]
    rows = refs[0].shape[0]
    for i, ref in enumerate(refs[:-1]):
        out_ref[i * rows : (i + 1) * rows] = ref[...]


def stack(*arrays):
    rows, width = arrays[0].shape
    shape = (len(arrays) * rows, width)
    return pl.pallas_call(
        stack_kernel,
        grid=(1,),
        in_specs=[whole((rows, width))] * len(arrays),
        out_specs=whole(shape),
        out_shape=jax.ShapeDtypeStruct(shape, BF),
        compiler_params=params(),
        cost_estimate=SMALL,
        name="stack",
    )(*arrays)


def head_norm(raw, factor):
    n = raw.shape[1]
    row = lax.broadcasted_iota(jnp.int32, (n, n), 0) // HEAD_DIM
    column = lax.broadcasted_iota(jnp.int32, (n, n), 1) // HEAD_DIM
    mean_of_head = jnp.where(row == column, 1.0 / HEAD_DIM, 0.0).astype(BF)
    mean_square = jnp.dot((raw * raw).astype(BF), mean_of_head, preferred_element_type=F32)
    return (raw * (lax.rsqrt(mean_square + EPS) * factor)).astype(BF)


def project(x, weight):
    return jnp.dot(x, weight, preferred_element_type=F32)


def joined(refs):
    return jnp.concatenate([r[...] for r in refs], axis=0)


def weights_of(scores, keep):
    weights = jnp.exp2(scores)
    if keep is not None:
        weights = jnp.where(keep, weights, 0.0)
    return weights.astype(BF)


def attend_quad(query, key, value, ones, plan, put):
    low = lax.broadcasted_iota(jnp.int32, ones.shape, 1) < HEAD_DIM
    low_q = low[:HALF]
    zero = jnp.zeros(ones.shape, BF)
    zero_q = zero[:HALF]
    for pair in range(2):
        lanes = slice(pair * PAIR, (pair + 1) * PAIR)
        k, v = key[:, lanes], value[:, lanes]
        right_a = jnp.concatenate([jnp.where(low, v, zero), jnp.where(low, ones, zero)], axis=1)
        right_b = jnp.concatenate([jnp.where(low, zero, v), jnp.where(low, zero, ones)], axis=1)
        for part in range(2):
            rows = slice(part * HALF, (part + 1) * HALF)
            q = query[rows, lanes]
            left, right = [], []
            for begin, end, rule in plan[part]:
                keep = None
                if rule is not None:
                    shape = (HALF, end - begin)
                    i = part * HALF + lax.broadcasted_iota(jnp.int32, shape, 0)
                    keep = rule(i, begin + lax.broadcasted_iota(jnp.int32, shape, 1))
                for q_head, v_head in (
                    (jnp.where(low_q, q, zero_q), right_a),
                    (jnp.where(low_q, zero_q, q), right_b),
                ):
                    scores = lax.dot_general(q_head, k[begin:end], NT, preferred_element_type=F32)
                    left.append(weights_of(scores, keep))
                    right.append(v_head[begin:end])
            total = jnp.dot(
                jnp.concatenate(left, axis=1), jnp.concatenate(right, axis=0), preferred_element_type=F32
            )
            put(pair, rows, total)


def until(i, j):
    return j <= i


def upper_since(i, j):
    return (j >= UPPER) | (j >= i)


def first_lower_since(i, j):
    return (j < BLOCK + UPPER) | (j - BLOCK >= i)


FIRST_PLAN = (
    ((0, HALF, until), (BLOCK, 2 * BLOCK, None)),
    ((0, HALF, None), (HALF, BLOCK, until), (BLOCK, 2 * BLOCK, first_lower_since)),
)
FIRST_PLACES = (None, None, 0, 3)
FULL_PLAN = (((0, BLOCK, None),),) * 2
LAST_PLAN = (((0, BLOCK, upper_since),), ((HALF, BLOCK, upper_since),))


def keys_of(refs, w_k, w_v, valid_ref, valid):
    x = joined(refs)
    key = head_norm(project(x, joined(w_k)), 1.0)
    value = project(x, joined(w_v))
    values, ones, row = [], [], 0
    for ref, place in zip(refs, valid):
        rows = ref.shape[0]
        part, one = value[row : row + rows], jnp.ones((rows, PAIR), F32)
        if place is not None:
            counts = valid_ref[place] > 0
            part, one = jnp.where(counts, part, 0.0), jnp.where(counts, one, 0.0)
        values.append(part.astype(BF))
        ones.append(one.astype(BF))
        row += rows
    return key, jnp.concatenate(values, axis=0), jnp.concatenate(ones, axis=0)


def first_kernel(*refs):
    n = len(FIRST_PLACES)
    valid_ref, rows = refs[0], refs[1 : 1 + n]
    w_q, w_k, w_v = refs[1 + n : 9 + n], refs[9 + n : 17 + n], refs[17 + n : 25 + n]
    query_ref, total_ref, token_ref = refs[25 + n :]
    token_ref[...] = jnp.zeros_like(token_ref)
    query = head_norm(project(joined(rows[:2]), joined(w_q)), QUERY_FACTOR)
    query_ref[...] = query

    def put(pair, rows, total):
        total_ref[pair, rows, :] = total

    attend_quad(query, *keys_of(rows, w_k, w_v, valid_ref, FIRST_PLACES), FIRST_PLAN, put)


def step_kernel(plan, valid, *refs):
    n = len(valid)
    valid_ref, rows = refs[0], refs[1 : 1 + n]
    w_k, w_v = refs[1 + n : 9 + n], refs[9 + n : 17 + n]
    query_ref, total_ref, _, out_ref, token_ref = refs[17 + n :]
    token_ref[...] = jnp.zeros_like(token_ref)

    def put(pair, rows, total):
        out_ref[pair, rows, :] = total_ref[pair, rows, :] + total

    attend_quad(query_ref[...], *keys_of(rows, w_k, w_v, valid_ref, valid), plan, put)


def last_kernel(plan, valid, *refs):
    n = len(valid)
    valid_ref, order_ref, rows = refs[0], refs[1], refs[2 : 2 + n]
    w_k, w_v, w_out = refs[2 + n : 10 + n], refs[10 + n : 18 + n], refs[18 + n : 26 + n]
    query_ref, total_ref, _, out_ref, context = refs[26 + n :]
    g = pl.program_id(0)

    def put(pair, rows, total):
        total = total_ref[pair, rows, :] + total
        context[2 * g + pair, rows, :] = (total[:, :PAIR] / total[:, PAIR:]).astype(BF)

    attend_quad(query_ref[...], *keys_of(rows, w_k, w_v, valid_ref, valid), plan, put)

    @pl.when(g == pl.num_programs(0) - 1)
    def _():
        x = jnp.concatenate([context[order_ref[r]] for r in range(8)], axis=1)
        out_ref[...] = project(x, joined(w_out)).astype(BF)


def weight_arrays(parts, kind):
    return [part[kind][0] for part in parts]


def weight_specs(parts, kind):
    return [pl.BlockSpec((PAIR, QUAD), functools.partial(lambda row, g: (row, g), part[kind][1])) for part in parts]


QUERY_SPEC = pl.BlockSpec((BLOCK, QUAD), lambda g: (0, g))
TOTAL_SPEC = pl.BlockSpec((2, BLOCK, QUAD), lambda g: (g, 0, 0))


def attend_first(valid, rows, parts):
    width = rows[0].shape[1]
    return pl.pallas_call(
        first_kernel,
        grid=(width // QUAD,),
        in_specs=[SMEM_WHOLE]
        + [whole(x.shape) for x in rows]
        + weight_specs(parts, 0)
        + weight_specs(parts, 1)
        + weight_specs(parts, 2),
        out_specs=[QUERY_SPEC, TOTAL_SPEC, whole(TOKEN.shape)],
        out_shape=[
            jax.ShapeDtypeStruct((BLOCK, width), BF),
            jax.ShapeDtypeStruct((width // PAIR, BLOCK, QUAD), F32),
            TOKEN,
        ],
        compiler_params=params(),
        cost_estimate=SMALL,
        name="first",
    )(valid, *rows, *(w for kind in range(3) for w in weight_arrays(parts, kind)))


def attend_step(plan, places, valid, rows, parts, query, total, token):
    width = rows[0].shape[1]
    return pl.pallas_call(
        functools.partial(step_kernel, plan, places),
        grid=(width // QUAD,),
        in_specs=[SMEM_WHOLE]
        + [whole(x.shape) for x in rows]
        + weight_specs(parts, 1)
        + weight_specs(parts, 2)
        + [QUERY_SPEC, TOTAL_SPEC, pl.BlockSpec(memory_space=pl.ANY)],
        out_specs=[TOTAL_SPEC, whole(TOKEN.shape)],
        out_shape=[jax.ShapeDtypeStruct(total.shape, F32), TOKEN],
        compiler_params=params(),
        cost_estimate=SMALL,
        name="step",
    )(valid, *rows, *weight_arrays(parts, 1), *weight_arrays(parts, 2), query, total, token)


def attend_last(plan, places, valid, order, rows, parts, query, total, token):
    width = rows[0].shape[1]
    return pl.pallas_call(
        functools.partial(last_kernel, plan, places),
        grid=(width // QUAD,),
        in_specs=[SMEM_WHOLE] * 2
        + [whole(x.shape) for x in rows]
        + weight_specs(parts, 1)
        + weight_specs(parts, 2)
        + [
            pl.BlockSpec((PAIR, width), functools.partial(lambda row, g: (row, 0), part[3][1])) for part in parts
        ]
        + [QUERY_SPEC, TOTAL_SPEC, pl.BlockSpec(memory_space=pl.ANY)],
        out_specs=whole((BLOCK, width)),
        out_shape=jax.ShapeDtypeStruct((BLOCK, width), BF),
        scratch_shapes=[pltpu.VMEM((width // PAIR, BLOCK, PAIR), BF)],
        compiler_params=params(),
        cost_estimate=SMALL,
        name="last",
    )(valid, order, *rows, *(w for kind in (1, 2, 3) for w in weight_arrays(parts, kind)), query, total, token)


def along_seq(block, distance):
    count = lax.axis_size("seq")
    return lax.ppermute(block, "seq", [(i, (i + distance) % count) for i in range(count)])


def over_fsdp(block, dy, other):
    count = lax.axis_size("fsdp")
    return lax.ppermute(block, "fsdp", [(i, (i // 2 * 2 + 2 * dy) % count + (i + other) % 2) for i in range(count)])


def together(*arrays):
    return lax.optimization_barrier(arrays)


def weight_order():
    me = lax.axis_index("fsdp")
    y, core = me // 2, me % 2
    return jnp.stack(
        [2 * ((y + dy) % 4) + (core + other) % 2 for dy in (0, 3, 1, 2) for other in (0, 1)]
    ).astype(jnp.int32)


def local(byte_states, group_states, boundaries, w_query, w_key, w_value, w_out):
    own_bytes, own_groups, starts = byte_states[0], group_states[0], boundaries[0]
    rows, width = own_bytes.shape
    owned = own_groups.shape[0]
    position = lax.axis_index("seq")
    order = weight_order()
    valid = jnp.stack([position >= k for k in range(1, 5)]).astype(jnp.int32)

    tail, *own_weights = together(own_groups[owned - TAIL :], w_query, w_key, w_value, w_out)
    carried = along_seq(tail, 1)
    packed = stack(*own_weights)
    half = packed.shape[0] // 2
    below, above = over_fsdp(packed, 1, 0), over_fsdp(packed, -1, 0)
    far = over_fsdp(below[:half], 1, 0), over_fsdp(above[half:], -1, 0)

    never = jnp.int32(2**30)
    padded = jnp.concatenate([jnp.zeros((TAIL,), jnp.int32), starts, jnp.full((1,), never, jnp.int32)])
    window = lax.dynamic_slice_in_dim(padded, position * owned, owned + TAIL + 1, 0) - position * rows
    begin, end = window[:-1], window[1:]
    gap = jnp.full((PAIR - TAIL,), never, jnp.int32)
    window = jnp.stack([jnp.concatenate([w[:TAIL], gap, w[TAIL:]]) for w in (begin, end)])

    order, valid = together(order, valid)
    dechunked, upper, lower = prep(order, window, own_bytes, carried, own_groups)

    up, down = {1: along_seq(upper, 1)}, {4: along_seq(lower, 4)}
    *far, up[1], down[4] = together(*far, up[1], down[4])
    parts = []
    for part in (packed, below, above):
        parts += [tuple((x, kind) for kind in range(4)) for x in (part, over_fsdp(part, 0, 1))]
    for a, b in (far, [over_fsdp(x, 0, 1) for x in far]):
        parts.append(((a, 0), (a, 1), (b, 0), (b, 1)))

    up[2], down[3] = along_seq(up[1], 1), along_seq(down[4], -1)
    query, total, token = attend_first(valid, (upper, lower, up[1], down[4]), parts)

    up[2], down[3], token = together(up[2], down[3], token)
    up[3], down[2] = along_seq(up[2], 1), along_seq(down[3], -1)
    total, token = attend_step(FULL_PLAN, (1, 2), valid, (up[2], down[3]), parts, query, total, token)

    up[3], down[2], token = together(up[3], down[2], token)
    up[4], down[1] = along_seq(up[3], 1), along_seq(down[2], -1)
    total, token = attend_step(FULL_PLAN, (2, 1), valid, (up[3], down[2]), parts, query, total, token)
    attended = attend_last(LAST_PLAN, (3, 0), valid, order, (up[4], down[1]), parts, query, total, token)
    return dechunked[None], attended[None]


def solution(mesh):
    placed = (P("fsdp", "seq", None),) * 2 + (P("fsdp", None),) * 5
    return jax.shard_map(
        local,
        mesh=mesh,
        in_specs=placed,
        out_specs=(P("fsdp", "seq", None), P("fsdp", "seq", None)),
        check_vma=False,
    )
```

```python
import functools

import jax
import jax.numpy as jnp
from jax import lax
from jax.experimental import pallas as pl
from jax.experimental.pallas import tpu as pltpu
from jax.sharding import PartitionSpec as P

HEAD_DIM = 64
TAIL = 64
PAIR = 2 * HEAD_DIM
QUAD = 2 * PAIR
HALF = 256
UPPER = 384
BLOCK = 512
EPS = 1e-6
QUERY_FACTOR = 16.0 / HEAD_DIM * 1.4426950408889634
BF = jnp.bfloat16
F32 = jnp.float32
VMEM_WHOLE = pl.BlockSpec(memory_space=pltpu.VMEM)
SMEM_WHOLE = pl.BlockSpec(memory_space=pltpu.SMEM)
SMALL = pl.CostEstimate(flops=1, bytes_accessed=1, transcendentals=0)
TOKEN = jax.ShapeDtypeStruct((8, 128), F32)
NT = (((1,), (1,)), ((), ()))
VMEM_LIMIT = 63 * 2**20


def params():
    return pltpu.CompilerParams(vmem_limit_bytes=VMEM_LIMIT)


def prep_kernel(order_ref, win_ref, bytes_ref, carried_ref, groups_ref, out_ref, upper_ref, lower_ref, hold):
    rows, width = bytes_ref.shape
    start, following = win_ref[0:1, :], win_ref[1:2, :]

    def one_hot(lo, hi):
        position = lax.broadcasted_iota(jnp.int32, (rows, hi - lo), 0)
        return ((start[:, lo:hi] <= position) & (following[:, lo:hi] > position)).astype(F32).astype(BF)

    own = groups_ref.shape[0]
    lifted = jnp.dot(one_hot(PAIR, PAIR + own), groups_ref[...], preferred_element_type=F32)
    lifted += jnp.dot(one_hot(0, TAIL), carried_ref[...], preferred_element_type=F32)
    dechunked = (bytes_ref[...].astype(F32) + lifted).astype(BF)
    out_ref[...] = dechunked
    wide = dechunked.astype(F32)
    mean = jnp.sum(wide * wide, axis=-1, keepdims=True) * (1.0 / width)
    hold[...] = (wide * lax.rsqrt(mean + EPS)).astype(BF)
    for r in range(width // PAIR):
        at = pl.multiple_of(order_ref[r] * PAIR, PAIR)
        upper_ref[:, r * PAIR : (r + 1) * PAIR] = hold[:UPPER, pl.ds(at, PAIR)]
        lower_ref[:, r * PAIR : (r + 1) * PAIR] = hold[UPPER:, pl.ds(at, PAIR)]


def whole(shape):
    return pl.BlockSpec(shape, lambda *_: (0,) * len(shape))


def prep(order, window, own_bytes, carried, own_groups):
    rows, width = own_bytes.shape
    shapes = [(rows, width), (UPPER, width), (rows - UPPER, width)]
    return pl.pallas_call(
        prep_kernel,
        grid=(1,),
        in_specs=[SMEM_WHOLE] + [whole(x.shape) for x in (window, own_bytes, carried, own_groups)],
        out_specs=[whole(shape) for shape in shapes],
        out_shape=[jax.ShapeDtypeStruct(shape, BF) for shape in shapes],
        scratch_shapes=[pltpu.VMEM((rows, width), BF)],
        compiler_params=params(),
        cost_estimate=SMALL,
        name="prep",
    )(order, window, own_bytes, carried, own_groups)


def stack_kernel(*refs):
    out_ref = refs[-1]
    rows = refs[0].shape[0]
    for i, ref in enumerate(refs[:-1]):
        out_ref[i * rows : (i + 1) * rows] = ref[...]


def stack(*arrays):
    rows, width = arrays[0].shape
    shape = (len(arrays) * rows, width)
    return pl.pallas_call(
        stack_kernel,
        grid=(1,),
        in_specs=[whole((rows, width))] * len(arrays),
        out_specs=whole(shape),
        out_shape=jax.ShapeDtypeStruct(shape, BF),
        compiler_params=params(),
        cost_estimate=SMALL,
        name="stack",
    )(*arrays)


def head_norm(raw, factor):
    n = raw.shape[1]
    row = lax.broadcasted_iota(jnp.int32, (n, n), 0) // HEAD_DIM
    column = lax.broadcasted_iota(jnp.int32, (n, n), 1) // HEAD_DIM
    mean_of_head = jnp.where(row == column, 1.0 / HEAD_DIM, 0.0).astype(BF)
    mean_square = jnp.dot((raw * raw).astype(BF), mean_of_head, preferred_element_type=F32)
    return (raw * (lax.rsqrt(mean_square + EPS) * factor)).astype(BF)


def project(x, weight):
    return jnp.dot(x, weight, preferred_element_type=F32)


def joined(refs):
    return jnp.concatenate([r[...] for r in refs], axis=0)


def weights_of(scores, keep):
    weights = jnp.exp2(scores)
    if keep is not None:
        weights = jnp.where(keep, weights, 0.0)
    return weights.astype(BF)


def attend_quad(query, key, value, ones, plan, put):
    low = lax.broadcasted_iota(jnp.int32, ones.shape, 1) < HEAD_DIM
    low_q = low[:HALF]
    zero = jnp.zeros(ones.shape, BF)
    zero_q = zero[:HALF]
    for pair in range(2):
        lanes = slice(pair * PAIR, (pair + 1) * PAIR)
        k, v = key[:, lanes], value[:, lanes]
        right_a = jnp.concatenate([jnp.where(low, v, zero), jnp.where(low, ones, zero)], axis=1)
        right_b = jnp.concatenate([jnp.where(low, zero, v), jnp.where(low, zero, ones)], axis=1)
        for part in range(2):
            rows = slice(part * HALF, (part + 1) * HALF)
            q = query[rows, lanes]
            left, right = [], []
            for begin, end, rule in plan[part]:
                keep = None
                if rule is not None:
                    shape = (HALF, end - begin)
                    i = part * HALF + lax.broadcasted_iota(jnp.int32, shape, 0)
                    keep = rule(i, begin + lax.broadcasted_iota(jnp.int32, shape, 1))
                for q_head, v_head in (
                    (jnp.where(low_q, q, zero_q), right_a),
                    (jnp.where(low_q, zero_q, q), right_b),
                ):
                    scores = lax.dot_general(q_head, k[begin:end], NT, preferred_element_type=F32)
                    left.append(weights_of(scores, keep))
                    right.append(v_head[begin:end])
            total = jnp.dot(
                jnp.concatenate(left, axis=1), jnp.concatenate(right, axis=0), preferred_element_type=F32
            )
            put(pair, rows, total)


def until(i, j):
    return j <= i


def upper_since(i, j):
    return (j >= UPPER) | (j >= i)


def middle_since(i, j):
    return (j < UPPER) | (j >= BLOCK) | (j >= i)


FIRST_PLAN = (
    ((0, HALF, until), (BLOCK, BLOCK + UPPER, None)),
    ((0, HALF, None), (HALF, BLOCK, until), (BLOCK, BLOCK + UPPER, None)),
)
FIRST_PLACES = (None, None, 0)
SECOND_PLAN = (((0, 2 * BLOCK - UPPER, None),), ((0, 2 * BLOCK - UPPER, middle_since),))
FULL_PLAN = (((0, BLOCK, None),),) * 2
LAST_PLAN = (((0, BLOCK, upper_since),), ((HALF, BLOCK, upper_since),))


def keys_of(refs, w_k, w_v, valid_ref, valid):
    x = joined(refs)
    key = head_norm(project(x, joined(w_k)), 1.0)
    value = project(x, joined(w_v))
    values, ones, row = [], [], 0
    for ref, place in zip(refs, valid):
        rows = ref.shape[0]
        part, one = value[row : row + rows], jnp.ones((rows, PAIR), F32)
        if place is not None:
            counts = valid_ref[place] > 0
            part, one = jnp.where(counts, part, 0.0), jnp.where(counts, one, 0.0)
        values.append(part.astype(BF))
        ones.append(one.astype(BF))
        row += rows
    return key, jnp.concatenate(values, axis=0), jnp.concatenate(ones, axis=0)


def first_kernel(*refs):
    n = len(FIRST_PLACES)
    valid_ref, rows = refs[0], refs[1 : 1 + n]
    w_q, w_k, w_v = refs[1 + n : 9 + n], refs[9 + n : 17 + n], refs[17 + n : 25 + n]
    query_ref, total_ref, token_ref = refs[25 + n :]
    token_ref[...] = jnp.zeros_like(token_ref)
    query = head_norm(project(joined(rows[:2]), joined(w_q)), QUERY_FACTOR)
    query_ref[...] = query

    def put(pair, rows, total):
        total_ref[pair, rows, :] = total

    attend_quad(query, *keys_of(rows, w_k, w_v, valid_ref, FIRST_PLACES), FIRST_PLAN, put)


def step_kernel(plan, valid, *refs):
    n = len(valid)
    valid_ref, rows = refs[0], refs[1 : 1 + n]
    w_k, w_v = refs[1 + n : 9 + n], refs[9 + n : 17 + n]
    query_ref, total_ref, _, out_ref, token_ref = refs[17 + n :]
    token_ref[...] = jnp.zeros_like(token_ref)

    def put(pair, rows, total):
        out_ref[pair, rows, :] = total_ref[pair, rows, :] + total

    attend_quad(query_ref[...], *keys_of(rows, w_k, w_v, valid_ref, valid), plan, put)


def last_kernel(plan, valid, *refs):
    n = len(valid)
    valid_ref, order_ref, rows = refs[0], refs[1], refs[2 : 2 + n]
    w_k, w_v, w_out = refs[2 + n : 10 + n], refs[10 + n : 18 + n], refs[18 + n : 26 + n]
    query_ref, total_ref, _, out_ref, context = refs[26 + n :]
    g = pl.program_id(0)

    def put(pair, rows, total):
        total = total_ref[pair, rows, :] + total
        context[2 * g + pair, rows, :] = (total[:, :PAIR] / total[:, PAIR:]).astype(BF)

    attend_quad(query_ref[...], *keys_of(rows, w_k, w_v, valid_ref, valid), plan, put)

    @pl.when(g == pl.num_programs(0) - 1)
    def _():
        x = jnp.concatenate([context[order_ref[r]] for r in range(8)], axis=1)
        out_ref[...] = project(x, joined(w_out)).astype(BF)


def weight_arrays(parts, kind):
    return [part[kind][0] for part in parts]


def weight_specs(parts, kind):
    return [pl.BlockSpec((PAIR, QUAD), functools.partial(lambda row, g: (row, g), part[kind][1])) for part in parts]


QUERY_SPEC = pl.BlockSpec((BLOCK, QUAD), lambda g: (0, g))
TOTAL_SPEC = pl.BlockSpec((2, BLOCK, QUAD), lambda g: (g, 0, 0))


def attend_first(valid, rows, parts):
    width = rows[0].shape[1]
    return pl.pallas_call(
        first_kernel,
        grid=(width // QUAD,),
        in_specs=[SMEM_WHOLE]
        + [whole(x.shape) for x in rows]
        + weight_specs(parts, 0)
        + weight_specs(parts, 1)
        + weight_specs(parts, 2),
        out_specs=[QUERY_SPEC, TOTAL_SPEC, whole(TOKEN.shape)],
        out_shape=[
            jax.ShapeDtypeStruct((BLOCK, width), BF),
            jax.ShapeDtypeStruct((width // PAIR, BLOCK, QUAD), F32),
            TOKEN,
        ],
        compiler_params=params(),
        cost_estimate=SMALL,
        name="first",
    )(valid, *rows, *(w for kind in range(3) for w in weight_arrays(parts, kind)))


def attend_step(plan, places, valid, rows, parts, query, total, token):
    width = rows[0].shape[1]
    return pl.pallas_call(
        functools.partial(step_kernel, plan, places),
        grid=(width // QUAD,),
        in_specs=[SMEM_WHOLE]
        + [whole(x.shape) for x in rows]
        + weight_specs(parts, 1)
        + weight_specs(parts, 2)
        + [QUERY_SPEC, TOTAL_SPEC, pl.BlockSpec(memory_space=pl.ANY)],
        out_specs=[TOTAL_SPEC, whole(TOKEN.shape)],
        out_shape=[jax.ShapeDtypeStruct(total.shape, F32), TOKEN],
        compiler_params=params(),
        cost_estimate=SMALL,
        name="step",
    )(valid, *rows, *weight_arrays(parts, 1), *weight_arrays(parts, 2), query, total, token)


def attend_last(plan, places, valid, order, rows, parts, query, total, token):
    width = rows[0].shape[1]
    return pl.pallas_call(
        functools.partial(last_kernel, plan, places),
        grid=(width // QUAD,),
        in_specs=[SMEM_WHOLE] * 2
        + [whole(x.shape) for x in rows]
        + weight_specs(parts, 1)
        + weight_specs(parts, 2)
        + [
            pl.BlockSpec((PAIR, width), functools.partial(lambda row, g: (row, 0), part[3][1])) for part in parts
        ]
        + [QUERY_SPEC, TOTAL_SPEC, pl.BlockSpec(memory_space=pl.ANY)],
        out_specs=whole((BLOCK, width)),
        out_shape=jax.ShapeDtypeStruct((BLOCK, width), BF),
        scratch_shapes=[pltpu.VMEM((width // PAIR, BLOCK, PAIR), BF)],
        compiler_params=params(),
        cost_estimate=SMALL,
        name="last",
    )(valid, order, *rows, *(w for kind in (1, 2, 3) for w in weight_arrays(parts, kind)), query, total, token)


def along_seq(block, distance):
    count = lax.axis_size("seq")
    return lax.ppermute(block, "seq", [(i, (i + distance) % count) for i in range(count)])


def over_fsdp(block, dy, other):
    count = lax.axis_size("fsdp")
    return lax.ppermute(block, "fsdp", [(i, (i // 2 * 2 + 2 * dy) % count + (i + other) % 2) for i in range(count)])


def together(*arrays):
    return lax.optimization_barrier(arrays)


def weight_order():
    me = lax.axis_index("fsdp")
    y, core = me // 2, me % 2
    return jnp.stack(
        [2 * ((y + dy) % 4) + (core + other) % 2 for dy in (0, 3, 1, 2) for other in (0, 1)]
    ).astype(jnp.int32)


def local(byte_states, group_states, boundaries, w_query, w_key, w_value, w_out):
    own_bytes, own_groups, starts = byte_states[0], group_states[0], boundaries[0]
    rows, width = own_bytes.shape
    owned = own_groups.shape[0]
    position = lax.axis_index("seq")
    order = weight_order()
    valid = jnp.stack([position >= k for k in range(1, 5)]).astype(jnp.int32)

    tail, *own_weights = together(own_groups[owned - TAIL :], w_query, w_key, w_value, w_out)
    carried = along_seq(tail, 1)
    packed = stack(*own_weights)
    half = packed.shape[0] // 2
    below, above = over_fsdp(packed, 1, 0), over_fsdp(packed, -1, 0)
    far = over_fsdp(below[:half], 1, 0), over_fsdp(above[half:], -1, 0)

    never = jnp.int32(2**30)
    padded = jnp.concatenate([jnp.zeros((TAIL,), jnp.int32), starts, jnp.full((1,), never, jnp.int32)])
    window = lax.dynamic_slice_in_dim(padded, position * owned, owned + TAIL + 1, 0) - position * rows
    begin, end = window[:-1], window[1:]
    gap = jnp.full((PAIR - TAIL,), never, jnp.int32)
    window = jnp.stack([jnp.concatenate([w[:TAIL], gap, w[TAIL:]]) for w in (begin, end)])

    order, valid = together(order, valid)
    dechunked, upper, lower = prep(order, window, own_bytes, carried, own_groups)

    up, down = {1: along_seq(upper, 1)}, {4: along_seq(lower, 4)}
    *far, up[1], down[4] = together(*far, up[1], down[4])
    parts = []
    for part in (packed, below, above):
        parts += [tuple((x, kind) for kind in range(4)) for x in (part, over_fsdp(part, 0, 1))]
    for a, b in (far, [over_fsdp(x, 0, 1) for x in far]):
        parts.append(((a, 0), (a, 1), (b, 0), (b, 1)))

    up[2], down[3] = along_seq(up[1], 1), along_seq(down[4], -1)
    query, total, token = attend_first(valid, (upper, lower, up[1]), parts)

    up[2], down[3], token = together(up[2], down[3], token)
    up[3], down[2] = along_seq(up[2], 1), along_seq(down[3], -1)
    rows = (up[2], down[4], down[3])
    total, token = attend_step(SECOND_PLAN, (1, 3, 2), valid, rows, parts, query, total, token)

    up[3], down[2], token = together(up[3], down[2], token)
    up[4], down[1] = along_seq(up[3], 1), along_seq(down[2], -1)
    total, token = attend_step(FULL_PLAN, (2, 1), valid, (up[3], down[2]), parts, query, total, token)
    attended = attend_last(LAST_PLAN, (3, 0), valid, order, (up[4], down[1]), parts, query, total, token)
    return dechunked[None], attended[None]


def solution(mesh):
    placed = (P("fsdp", "seq", None),) * 2 + (P("fsdp", None),) * 5
    return jax.shard_map(
        local,
        mesh=mesh,
        in_specs=placed,
        out_specs=(P("fsdp", "seq", None), P("fsdp", "seq", None)),
        check_vma=False,
    )
```
